32 devices in a mesh: row: 8 (over z, x), col: 4 (over y, core).
Axes of the slice: x: 2, y: 2, z: 4, core: 2. Of those that a mesh axis runs over, the one named last changes fastest.
Arguments:
- inputs: bfloat16 [1024, 6144], P('col', 'row'), may hold values from -6 to 6
- out_grad: bfloat16 [1024, 6144], P('col', 'row'), may hold values from -6 to 6
- pre_act: bfloat16 [1024, 24576], P('row', 'col'), may hold values from -8 to 8
- w_in: bfloat16 [6144, 24576], P('row', 'col'), may hold values from -0.078125 to 0.078125
- w_out: bfloat16 [24576, 6144], P('col', 'row'), may hold values from -0.0390625 to 0.0390625
Outputs:
- in_grad: bfloat16 [1024, 6144], P('col', 'row')
- w_in_grad: bfloat16 [6144, 24576], P('row', 'col')
- w_out_grad: bfloat16 [24576, 6144], P('col', 'row')
The draws below stay inside these ranges and needn't reach their ends.
All inputs are finite; a program needn't handle non-finite values.
Results may differ from the reference program's by a relative error of at most 0.03.
Values may be sent and summed in bfloat16 or wider, within the bound.
A program may use at most 128 MiB of HBM per device.

```python
import jax
import jax.numpy as jnp
from jax import lax

D = 6144
FF = 24576
TOKENS = 1024
N_ROW = 8


def with_spikes(drawn, stream_key, source, target, shards_of, factor):
    def block_of(axis_at):
        return (jnp.arange(drawn.shape[axis_at]) // (drawn.shape[axis_at] // shards_of)).reshape((-1,) + (1,) * (drawn.ndim - 1 - axis_at))

    near = jax.random.permutation(stream_key, shards_of)[block_of(target)]
    second = (block_of(target) + shards_of // 2) % shards_of
    return jnp.where((block_of(source) == near) | (block_of(source) == second), factor * drawn, drawn)


def steps_of(stream_key, shape, cuts, low, largest):
    loudness, own = 1.0, jax.random.fold_in(stream_key, 6)
    for dim, blocks in cuts:
        draws = jnp.exp(jax.random.uniform(jax.random.fold_in(own, dim), (blocks,), jnp.float32, low / len(cuts), largest / len(cuts)))
        loudness = loudness * jnp.repeat(draws, shape[dim] // blocks).reshape([-1 if axis == dim else 1 for axis in range(len(shape))])
    return loudness


def scatter_about(stream_key, shape, spread, bound, cuts=(), held_as=jnp.bfloat16):
    drawn = spread * jax.random.normal(stream_key, shape, jnp.float32)
    if cuts:
        drawn = drawn * steps_of(stream_key, shape, cuts, -0.22, 0.18)
    return jnp.clip(drawn, -bound, bound).astype(held_as)


def bell_draw_with(stream_key, dims, width, limit, pieces, heavy, held_as=jnp.bfloat16):
    array = width * jax.random.normal(stream_key, dims, jnp.float32)
    if pieces:
        array = array * steps_of(stream_key, dims, pieces, -0.22, 0.18)
    return jnp.clip(with_spikes(array, jax.random.fold_in(stream_key, 3), *heavy), -limit, limit).astype(held_as)


def setup_inputs(seed: int = 0) -> dict:
    arg_keys = jax.random.split(jax.random.key(seed), 6)
    inputs = scatter_about(arg_keys[0], (TOKENS, D), 1.0, 6.0, ((0, 4), (1, 8)))
    out_grad = bell_draw_with(arg_keys[1], (TOKENS, D), 1.0, 6.0, ((0, 4), (1, 8)), (1, 0, 8, 2.0))
    pre_act = scatter_about(arg_keys[2], (TOKENS, FF), 1.5, 8.0, ((0, 8), (1, 4)))
    w_in = scatter_about(arg_keys[3], (D, FF), D ** -0.5, 0.078125, ((0, 8), (1, 4)))
    w_out = scatter_about(arg_keys[4], (FF, D), FF ** -0.5, 0.0390625, ((0, 4), (1, 8)))
    return dict(inputs=inputs, out_grad=out_grad, pre_act=pre_act, w_in=w_in, w_out=w_out)


def gelu_parts(pre_act):
    value = pre_act.astype(jnp.float32)
    cumul = 0.5 * (1.0 + jax.scipy.special.erf(value * 0.7071067811865476))
    density = jnp.exp(-0.5 * value * value) * 0.3989422804014327
    return value * cumul, cumul + value * density


def reference(inputs, out_grad, pre_act, w_in, w_out):
    value, slope = gelu_parts(pre_act)
    hidden = value.astype(jnp.bfloat16)
    width_block = out_grad.shape[1] // N_ROW
    hidden_grad = jnp.zeros((out_grad.shape[0], w_out.shape[0]), jnp.float32)
    for block_index in range(N_ROW):
        lower = block_index * width_block
        grad_block = out_grad[:, lower:lower + width_block]
        weight_block = w_out[:, lower:lower + width_block]
        partial_sum = jnp.dot(grad_block, weight_block.T, preferred_element_type=jnp.float32).astype(jnp.bfloat16)
        partial_sum = lax.optimization_barrier(partial_sum)
        hidden_grad = hidden_grad + partial_sum.astype(jnp.float32)
    pre_grad = (hidden_grad * slope).astype(jnp.bfloat16)
    w_out_grad = jnp.dot(hidden.T, out_grad, preferred_element_type=jnp.float32).astype(jnp.bfloat16)
    w_in_grad = jnp.dot(inputs.T, pre_grad, preferred_element_type=jnp.float32).astype(jnp.bfloat16)
    in_grad = jnp.dot(pre_grad, w_in.T, preferred_element_type=jnp.float32).astype(jnp.bfloat16)
    return in_grad, w_in_grad, w_out_grad
```

```python
import functools

import jax
import jax.numpy as jnp
from jax import lax
from jax.experimental import pallas as pl
from jax.experimental.pallas import tpu as pltpu
from jax.sharding import PartitionSpec as P

MESH = pl.DeviceIdType.MESH
CHIPS_Z = 4
PIECES = 2
TILE = 512


def gelu_parts(pre_act):
    value = pre_act.astype(jnp.float32)
    cumul = 0.5 * (1.0 + jax.scipy.special.erf(value * 0.7071067811865476))
    density = jnp.exp(-0.5 * value * value) * 0.3989422804014327
    return (value * cumul, cumul + value * density)


def row_at(place, n_row):
    across = n_row // CHIPS_Z
    x, z = place // CHIPS_Z, place % CHIPS_Z
    z = z + (x % 2) * (CHIPS_Z - 1 - 2 * z)
    return z * across + x


def place_of(row, n_row):
    across = n_row // CHIPS_Z
    x, z = row % across, row // across
    return x * CHIPS_Z + z + (x % 2) * (CHIPS_Z - 1 - 2 * z)


def ring_kernel(
    n_row, n_col,
    hid_ref, slope_ref, og_ref, in_ref, wout_ref,
    hid_all, pg_all, g_all, i_all,
    wv, gv, part, rbuf, pgv, sv,
    local_sem, csend, crecv, hsend, hrecv, rsend, rrecv, psend, precv,
):
    row, col = lax.axis_index("row"), lax.axis_index("col")
    place = place_of(row, n_row)
    ahead = row_at((place + 1) % n_row, n_row)
    behind = row_at((place + n_row - 1) % n_row, n_row)
    targets = (ahead, behind)
    tb, ff = hid_ref.shape
    tc = og_ref.shape[0]
    rw = tb // (2 * PIECES)
    steps = n_row - 1
    lanes = [(d, c) for c in range(PIECES) for d in range(2)]

    def block_at(d, s):
        at = (place + n_row - s) % n_row if d == 0 else (place + s) % n_row
        return row_at(at, n_row)

    def rows_of(block, d, c):
        return pl.ds(pl.multiple_of(block * tb + (d * PIECES + c) * rw, 16), rw)

    def own(d, c):
        return pl.ds((d * PIECES + c) * rw, rw)

    barrier = pltpu.get_barrier_semaphore()
    for target in targets:
        pl.semaphore_signal(barrier, 1, device_id=(target, col), device_id_type=MESH)
    for off in range(1, n_col):
        pl.semaphore_signal(
            barrier, 1, device_id=(row, (col + off) % n_col), device_id_type=MESH
        )
    pl.semaphore_wait(barrier, n_col + 1)

    def gather_copy(source, full, send, recv, d, c, s):
        block = block_at(d, s)
        src = source.at[own(d, c)] if source is not None else full.at[rows_of(block, d, c)]
        return pltpu.make_async_remote_copy(
            src_ref=src, dst_ref=full.at[rows_of(block, d, c)],
            send_sem=send.at[d, c, s], recv_sem=recv.at[d, c, s],
            device_id=(targets[d], col), device_id_type=MESH,
        )

    def sum_copy(d, c, s):
        block = block_at(d, s + 1)
        return pltpu.make_async_remote_copy(
            src_ref=part.at[rows_of(block, d, c)], dst_ref=rbuf.at[s, own(d, c)],
            send_sem=rsend.at[d, c, s], recv_sem=rrecv.at[d, c, s],
            device_id=(targets[d], col), device_id_type=MESH,
        )

    def col_copy(which, off):
        mine = pl.ds(pl.multiple_of(col * tc, 16), tc)
        return pltpu.make_async_remote_copy(
            src_ref=(og_ref, in_ref)[which], dst_ref=(gv, i_all)[which].at[mine],
            send_sem=csend.at[which, off - 1], recv_sem=crecv.at[which, off - 1],
            device_id=(row, (col + off) % n_col), device_id_type=MESH,
        )

    for d, c in lanes:
        gather_copy(hid_ref, hid_all, hsend, hrecv, d, c, 0).start()
    for which in range(2):
        for off in range(1, n_col):
            col_copy(which, off).start()
    mine = pl.ds(pl.multiple_of(col * tc, 16), tc)
    mine_row = pl.ds(pl.multiple_of(row * tb, 16), tb)
    local = [
        pltpu.make_async_copy(og_ref, gv.at[mine], local_sem.at[0]),
        pltpu.make_async_copy(wout_ref, wv, local_sem.at[1]),
        pltpu.make_async_copy(slope_ref, sv, local_sem.at[2]),
        pltpu.make_async_copy(in_ref, i_all.at[mine], local_sem.at[3]),
        pltpu.make_async_copy(hid_ref, hid_all.at[mine_row], local_sem.at[4]),
    ]
    for copy in local:
        copy.start()

    def hid_step(s):
        for d, c in lanes:
            gather_copy(None, hid_all, hsend, hrecv, d, c, s - 1).wait_recv()
            gather_copy(None, hid_all, hsend, hrecv, d, c, s).start()

    n_tiles = ff // TILE
    early = min(2, steps - 1)
    per_step = -(-n_tiles // (steps - 1 - early))

    @pl.loop(1, 1 + early)
    def _(s):
        hid_step(s)

    for copy in local:
        copy.wait()
    for which in range(2):
        for off in range(1, n_col):
            col_copy(which, off).wait_recv()

    g_out = pltpu.make_async_copy(gv, g_all, local_sem.at[5])
    g_out.start()

    def partial_tile(t):
        at = pl.ds(pl.multiple_of(t * TILE, TILE), TILE)
        part[:, at] = lax.dot_general(
            gv[...], wv[at, :], (((1,), (1,)), ((), ())), preferred_element_type=jnp.float32
        ).astype(jnp.bfloat16)

    @pl.loop(1 + early, steps)
    def _(s):
        hid_step(s)
        first = (s - 1 - early) * per_step

        @pl.loop(0, per_step)
        def _(k):
            @pl.when(first + k < n_tiles)
            def _():
                partial_tile(first + k)

    for d, c in lanes:
        sum_copy(d, c, 0).start()
    for d, c in lanes:
        gather_copy(None, hid_all, hsend, hrecv, d, c, steps - 1).wait_recv()

    @pl.loop(1, steps)
    def _(s):
        for d, c in lanes:
            sum_copy(d, c, s - 1).wait_recv()
            at = rows_of(block_at(d, s + 1), d, c)
            total = part[at, :].astype(jnp.float32) + rbuf[s - 1, own(d, c), :].astype(jnp.float32)
            part[at, :] = total.astype(jnp.bfloat16)
            sum_copy(d, c, s).start()

    for d, c in lanes:
        sum_copy(d, c, steps - 1).wait_recv()
        at = rows_of(row, d, c)
        total = part[at, :].astype(jnp.float32) + rbuf[steps - 1, own(d, c), :].astype(jnp.float32)
        pgv[own(d, c), :] = (total * sv[own(d, c), :]).astype(jnp.bfloat16)
        gather_copy(pgv, pg_all, psend, precv, d, c, 0).start()
    p_out = pltpu.make_async_copy(pgv, pg_all.at[mine_row], local_sem.at[6])
    p_out.start()

    @pl.loop(1, steps)
    def _(s):
        for d, c in lanes:
            gather_copy(None, pg_all, psend, precv, d, c, s - 1).wait_recv()
            gather_copy(None, pg_all, psend, precv, d, c, s).start()

    for d, c in lanes:
        gather_copy(None, pg_all, psend, precv, d, c, steps - 1).wait_recv()
    p_out.wait()
    g_out.wait()

    @pl.loop(0, steps)
    def _(s):
        for d, c in lanes:
            gather_copy(None, hid_all, hsend, hrecv, d, c, s).wait_send()
            sum_copy(d, c, s).wait_send()
            gather_copy(None, pg_all, psend, precv, d, c, s).wait_send()

    for which in range(2):
        for off in range(1, n_col):
            col_copy(which, off).wait_send()


def on_device(n_row, n_col, inputs, out_grad, pre_act, w_in, w_out):
    value, slope = gelu_parts(pre_act)
    hidden = value.astype(jnp.bfloat16)
    tb, ff = pre_act.shape
    tc, width = inputs.shape
    tokens, steps = tb * n_row, n_row - 1
    anywhere = pl.BlockSpec(memory_space=pl.ANY)
    lanes = pltpu.SemaphoreType.DMA((2, PIECES, steps))
    bf16 = jnp.bfloat16
    hidden_all, pre_grad, grad_all, inputs_all = pl.pallas_call(
        functools.partial(ring_kernel, n_row, n_col),
        out_shape=[
            jax.ShapeDtypeStruct((tokens, ff), bf16),
            jax.ShapeDtypeStruct((tokens, ff), bf16),
            jax.ShapeDtypeStruct((tokens, width), bf16),
            jax.ShapeDtypeStruct((tokens, width), bf16),
        ],
        in_specs=[anywhere] * 5,
        out_specs=[anywhere] * 4,
        scratch_shapes=[
            pltpu.VMEM((ff, width), bf16),
            pltpu.VMEM((tokens, width), bf16),
            pltpu.VMEM((tokens, ff), bf16),
            pltpu.VMEM((steps, tb, ff), bf16),
            pltpu.VMEM((tb, ff), bf16),
            pltpu.VMEM((tb, ff), jnp.float32),
            pltpu.SemaphoreType.DMA((7,)),
            pltpu.SemaphoreType.DMA((2, n_col - 1)),
            pltpu.SemaphoreType.DMA((2, n_col - 1)),
            lanes, lanes, lanes, lanes, lanes, lanes,
        ],
        compiler_params=pltpu.CompilerParams(
            collective_id=0, has_side_effects=True, vmem_limit_bytes=56 * 2**20
        ),
        name="ring",
    )(hidden, slope, out_grad, inputs, w_out)
    in_grad = lax.psum_scatter(
        lax.dot_general(
            pre_grad, w_in, (((1,), (1,)), ((), ())), preferred_element_type=jnp.float32
        ).astype(bf16),
        "col",
        scatter_dimension=0,
        tiled=True,
    )
    w_out_grad = lax.dot_general(
        hidden_all, grad_all, (((0,), (0,)), ((), ())), preferred_element_type=jnp.float32
    ).astype(bf16)
    w_in_grad = lax.dot_general(
        inputs_all, pre_grad, (((0,), (0,)), ((), ())), preferred_element_type=jnp.float32
    ).astype(bf16)
    return (in_grad, w_in_grad, w_out_grad)


def solution(mesh):
    in_specs = (P("col", "row"), P("col", "row"), P("row", "col"), P("row", "col"), P("col", "row"))
    out_specs = (P("col", "row"), P("row", "col"), P("col", "row"))
    return jax.shard_map(
        functools.partial(on_device, mesh.shape["row"], mesh.shape["col"]),
        mesh=mesh, in_specs=in_specs, out_specs=out_specs, check_vma=False,
    )
```
